128 devices in a mesh: group: 2 (over x_lo), sample: 16 (over z, x_hi, core), tensor: 4 (over y).
Axes of the slice: x: 4 (x_hi: 2, x_lo: 2; x = x_hi * 2 + x_lo), y: 4, z: 4, core: 2. Of those that a mesh axis runs over, the one named last changes fastest.
Arguments:
- resp_hidden: bfloat16 [32, 512, 5120], P(('group', 'sample')), parts along dimension 0, may hold values from -6 to 6
- prompt_hidden: bfloat16 [16384, 5120], P(('group', 'sample')), parts along dimension 0, may hold values from -6 to 6
- lengths: int32 [32], P(('group', 'sample')), parts along dimension 0, may hold values from 1 to 512, 5120 in all
- norm_gain: bfloat16 [5120], replicated, may hold values from 0.099609375 to 1.8984375
- wq: bfloat16 [5120, 2560], P('sample', 'tensor'), may hold values from -0.078125 to 0.078125
- wk: bfloat16 [5120, 512], P('sample', 'tensor'), may hold values from -0.078125 to 0.078125
- wv: bfloat16 [5120, 512], P('sample', 'tensor'), may hold values from -0.078125 to 0.078125
- q_bias: bfloat16 [2560], P('tensor'), may hold values from -12 to 12
- k_bias: bfloat16 [512], P('tensor'), may hold values from -12 to 12
- value_bias: bfloat16 [512], P('tensor'), may hold values from -3 to 3
- wo_t: bfloat16 [5120, 2560], P('sample', 'tensor'), may hold values from -0.5 to 0.5
- post_gain: bfloat16 [5120], replicated, may hold values from 0.099609375 to 1.8984375
Outputs:
- mixed: bfloat16 [32, 512, 5120], P(('group', 'sample')), parts along dimension 0
The draws below stay inside these ranges and needn't reach their ends.
There are 2 independent parts, one for each index of `group`. The reference program is written for one: setup_inputs(seed, part) draws one part's arguments, and reference() takes and returns one part's arrays. A program takes and returns all parts, laid end to end along the dimension named above; an argument that names none is the same for every part. Nothing has to cross between parts.
Inputs may be any that keep to these rules, and one draw needn't show every extreme that they name: The 16 lengths of each group sum to 5120 (the whole array, all groups together, sums to that times the number of groups); the longest response of each group has exactly 512 tokens.
All inputs are finite; a program needn't handle non-finite values.
Results may differ from the reference program's by a relative error of at most 0.017.
The reference program's roundings to bfloat16 on the way count: a program that leaves them out, or rounds other values in their place, can miss the bound.
Values may be sent and summed in bfloat16 or wider, within the bound.
A program may use at most 128 MiB of HBM per device.

```python
import math
import jax
import jax.numpy as jnp
import numpy as np
from jax import lax

MODEL_WIDTH = 5120
QUERY_HEADS = 20
KEY_VALUE_HEADS = 4
HEAD_SIZE = 128
RESPONSE_SLOTS = 512
GROUP_SAMPLES = 16
PROMPT_TOKENS = 8192
LEN_TOTAL = 5120


def draw_q_bias(key, part):
    key = jax.random.fold_in(key, 11)
    second_half = jax.random.fold_in(key, 1)
    return jnp.clip(0.5 * jax.random.normal(second_half, (QUERY_HEADS * HEAD_SIZE,), jnp.float32), -3.0, 3.0).astype(jnp.bfloat16)


def draw_k_bias(key, part):
    key = jax.random.fold_in(key, 23)
    second_half = jax.random.fold_in(key, 1)
    return jnp.clip(0.5 * jax.random.normal(second_half, (KEY_VALUE_HEADS * HEAD_SIZE,), jnp.float32), -3.0, 3.0).astype(jnp.bfloat16)


def level_of(rng, extent, shards, smallest, largest):
    level = 1.0
    for position, blocks in shards:
        draws = jax.random.uniform(jax.random.fold_in(jax.random.fold_in(rng, 6), position), (blocks,), jnp.float32, smallest / len(shards), largest / len(shards))
        level = level * jnp.repeat(jnp.exp(draws), extent[position] // blocks).reshape((-1,) + (1,) * (len(extent) - 1 - position))
    return level


def profile(count, total, most, lean):
    loads = [(1 << 20) // math.isqrt(grade ** lean) + 1 for grade in range(2, count + 1)]
    rest, given = total - most - (count - 1), [1] * (count - 1)
    while rest > 0:
        movable = [i for i in range(count - 1) if given[i] < most]
        whole, budget = sum([loads[i] for i in movable]), rest
        for i in movable:
            addition = min(most - given[i], max(1, budget * loads[i] // whole), rest)
            given[i] = given[i] + addition
            rest = rest - addition
    return np.array([most] + given)


def ragged_sizes(stream_key, amount, total, limit, skew):
    if amount == 2:
        one = jax.random.randint(stream_key, (), max(1, total - limit), min(limit, total - 1) + 1)
        return jnp.stack([one, total - one])
    sizes = jnp.asarray(profile(amount, total, limit, skew), jnp.int32)
    pairs = (amount - 1) // 2
    source_of, receiver = sizes[1:1 + 2 * pairs:2], sizes[2:2 + 2 * pairs:2]
    room = jnp.minimum(source_of - 1, limit - receiver)
    passed = jax.random.randint(jax.random.fold_in(stream_key, 1), (pairs,), 0, 1 << 20) % (room + 1)
    sizes = sizes.at[1:1 + 2 * pairs:2].set(source_of - passed).at[2:2 + 2 * pairs:2].set(receiver + passed)
    return sizes[jax.random.permutation(jax.random.fold_in(stream_key, 2), amount)]


def bell_draw(key, dims, deviation, most, cuts=(), held_as=jnp.bfloat16):
    result = jax.random.normal(key, dims, jnp.float32) * deviation
    if len(cuts) > 0:
        result = level_of(key, dims, cuts, -0.22, 0.18) * result
    return jnp.clip(result, min=-most, max=most).astype(held_as)


def setup_inputs(seed: int = 0, part: int = 0) -> dict:
    splits = jax.random.split(jax.random.key(seed), 13)
    part_keys = jax.random.split(jax.random.fold_in(splits[12], part), 13)
    resp_hidden = bell_draw(part_keys[0], (GROUP_SAMPLES, RESPONSE_SLOTS, MODEL_WIDTH), 1.0, 6.0, ((0, 16),))
    prompt_hidden = bell_draw(part_keys[1], (PROMPT_TOKENS, MODEL_WIDTH), 1.0, 6.0, ((0, 16),))
    lengths = ragged_sizes(part_keys[2], GROUP_SAMPLES, LEN_TOTAL, RESPONSE_SLOTS, 2).astype(jnp.int32)
    norm_gain = jnp.clip(1.0 + 0.18 * jax.random.normal(splits[3], (MODEL_WIDTH,), jnp.float32), 0.099609375, 1.8984375).astype(jnp.bfloat16)
    wq = bell_draw(splits[4], (MODEL_WIDTH, QUERY_HEADS * HEAD_SIZE), MODEL_WIDTH ** -0.5, 0.078125, ((0, 16), (1, 4)))
    wk = bell_draw(splits[5], (MODEL_WIDTH, KEY_VALUE_HEADS * HEAD_SIZE), MODEL_WIDTH ** -0.5, 0.078125, ((0, 16), (1, 4)))
    wv = bell_draw(splits[6], (MODEL_WIDTH, KEY_VALUE_HEADS * HEAD_SIZE), MODEL_WIDTH ** -0.5, 0.078125, ((0, 16), (1, 4)))
    q_bias = draw_q_bias(jax.random.fold_in(splits[12], 71), part)
    k_bias = draw_k_bias(jax.random.fold_in(splits[12], 71), part)
    value_bias = bell_draw(splits[9], (KEY_VALUE_HEADS * HEAD_SIZE,), 0.5, 3.0, ((0, 4),))
    wo_t = bell_draw(splits[10], (MODEL_WIDTH, QUERY_HEADS * HEAD_SIZE), (QUERY_HEADS * HEAD_SIZE // 16) ** -0.5, 0.5, ((0, 16), (1, 4)))
    post_gain = jnp.clip(1.0 + 0.18 * jax.random.normal(splits[11], (MODEL_WIDTH,), jnp.float32), 0.099609375, 1.8984375).astype(jnp.bfloat16)
    return {"resp_hidden": resp_hidden, "prompt_hidden": prompt_hidden, "lengths": lengths, "norm_gain": norm_gain, "wq": wq, "wk": wk, "wv": wv, "q_bias": q_bias, "k_bias": k_bias, "value_bias": value_bias, "wo_t": wo_t, "post_gain": post_gain}


EPS = 1e-06
THETA = 1000000.0

def normalize(rows, gain):
    values = rows.astype(jnp.float32)
    meansq = lax.optimization_barrier(jnp.mean(values * values, axis=-1, keepdims=True))
    return values * lax.rsqrt(meansq + EPS) * gain.astype(jnp.float32)

def rotary_embed(values, positions):
    half = values.shape[-1] // 2
    lanes = jnp.arange(half).astype(jnp.float32)
    inverse = THETA ** (-2.0 * lanes / values.shape[-1])
    angle = positions[:, None] * inverse[None, :]
    cosine = jnp.cos(angle)[:, None, :]
    sine = jnp.sin(angle)[:, None, :]
    first_half = values[..., :half]
    second_half = values[..., half:]
    return jnp.concatenate([first_half * cosine - second_half * sine, second_half * cosine + first_half * sine], axis=-1)

def reference(resp_hidden, prompt_hidden, lengths, norm_gain, wq, wk, wv, q_bias, k_bias, value_bias, wo_t, post_gain):
    f32 = jnp.float32
    to_brain_float = jnp.bfloat16
    flat = normalize(resp_hidden, norm_gain).astype(to_brain_float).reshape(GROUP_SAMPLES * RESPONSE_SLOTS, MODEL_WIDTH)
    prompt_normed = normalize(prompt_hidden, norm_gain).astype(to_brain_float)
    response_positions = (PROMPT_TOKENS + jnp.arange(RESPONSE_SLOTS)).astype(f32)
    prompt_positions = jnp.arange(PROMPT_TOKENS).astype(f32)
    q_raw = jnp.dot(flat, wq, preferred_element_type=f32) + q_bias.astype(f32)
    key_response = jnp.dot(flat, wk, preferred_element_type=f32) + k_bias.astype(f32)
    value_response = jnp.dot(flat, wv, preferred_element_type=f32) + value_bias.astype(f32)
    key_prompt = jnp.dot(prompt_normed, wk, preferred_element_type=f32) + k_bias.astype(f32)
    value_prompt = jnp.dot(prompt_normed, wv, preferred_element_type=f32) + value_bias.astype(f32)
    queries = rotary_embed(q_raw.reshape(GROUP_SAMPLES, RESPONSE_SLOTS, QUERY_HEADS, HEAD_SIZE), response_positions).astype(to_brain_float)
    response_keys = rotary_embed(key_response.reshape(GROUP_SAMPLES, RESPONSE_SLOTS, KEY_VALUE_HEADS, HEAD_SIZE), response_positions).astype(to_brain_float)
    response_values = value_response.reshape(GROUP_SAMPLES, RESPONSE_SLOTS, KEY_VALUE_HEADS, HEAD_SIZE).astype(to_brain_float)
    prompt_key_rows = rotary_embed(key_prompt.reshape(PROMPT_TOKENS, KEY_VALUE_HEADS, HEAD_SIZE), prompt_positions).astype(to_brain_float)
    prompt_value_rows = value_prompt.reshape(PROMPT_TOKENS, KEY_VALUE_HEADS, HEAD_SIZE).astype(to_brain_float)
    prefix_share = QUERY_HEADS // KEY_VALUE_HEADS
    scale = 1.0 / math.sqrt(HEAD_SIZE)
    column = jnp.arange(PROMPT_TOKENS + RESPONSE_SLOTS).astype(jnp.int32)
    rowpos = jnp.arange(RESPONSE_SLOTS).astype(jnp.int32)
    allowed = (column[None, :] < PROMPT_TOKENS) | (column[None, :] - PROMPT_TOKENS <= rowpos[:, None])

    def per_sample(args):
        q_sample, k_sample, v_sample = args

        def per_head(head):
            kv_head = head // prefix_share
            q_head = lax.dynamic_index_in_dim(q_sample, head, 1, keepdims=False)
            keys = jnp.concatenate([lax.dynamic_index_in_dim(prompt_key_rows, kv_head, 1, keepdims=False), lax.dynamic_index_in_dim(k_sample, kv_head, 1, keepdims=False)], 0)
            values = jnp.concatenate([lax.dynamic_index_in_dim(prompt_value_rows, kv_head, 1, keepdims=False), lax.dynamic_index_in_dim(v_sample, kv_head, 1, keepdims=False)], 0)
            score = jnp.dot(q_head, keys.T, preferred_element_type=f32) * scale
            score = jnp.where(allowed, score, -jnp.inf)
            highest = lax.optimization_barrier(jnp.max(score, axis=-1, keepdims=True))
            expd = jnp.exp(score - highest)
            denom = lax.optimization_barrier(jnp.sum(expd, axis=-1, keepdims=True))
            return jnp.dot(expd.astype(to_brain_float), values, preferred_element_type=f32) / denom
        return lax.map(per_head, jnp.arange(QUERY_HEADS).astype(jnp.int32))
    heads_out = lax.map(per_sample, (queries, response_keys, response_values))
    attended = heads_out.transpose(0, 2, 1, 3).reshape(GROUP_SAMPLES, RESPONSE_SLOTS, QUERY_HEADS * HEAD_SIZE)
    live = (jnp.arange(RESPONSE_SLOTS).astype(jnp.int32)[None, :] < lengths[:, None])[:, :, None]
    attended = jnp.where(live, attended, 0.0).astype(to_brain_float)
    branch = jnp.dot(attended.reshape(GROUP_SAMPLES * RESPONSE_SLOTS, QUERY_HEADS * HEAD_SIZE), wo_t.T, preferred_element_type=f32)
    resid = resp_hidden.astype(f32) + branch.reshape(GROUP_SAMPLES, RESPONSE_SLOTS, MODEL_WIDTH)
    mixed = normalize(resid, post_gain)
    return jnp.where(live, mixed, 0.0).astype(to_brain_float)
```

```python
import math

import jax
import jax.numpy as jnp
import numpy as np
from jax import lax
from jax.experimental import pallas as pl
from jax.experimental.pallas import tpu as pltpu
from jax.sharding import PartitionSpec as P

HEAD = 128
EPS = 1e-06
THETA = 1000000.0
WIDTH = 5120
ROWS = 512
Q_HEADS = 5
Q_COLS = Q_HEADS * HEAD
F32 = jnp.float32
BF16 = jnp.bfloat16
NT = (((1,), (1,)), ((), ()))
ALL = slice(None)


def rope_tables():
    half = np.arange(HEAD // 2, dtype=np.float64)
    inverse = THETA ** (-2.0 * half / HEAD)

    def pair(positions):
        angle = positions[:, None] * inverse[None, :]
        cosine, sine = np.cos(angle), np.sin(angle)
        both = np.concatenate([cosine, cosine], 1), np.concatenate([sine, sine], 1)
        return both[0].astype(np.float32), both[1].astype(np.float32)

    return pair(np.arange(ROWS, dtype=np.float64)) + pair(np.arange(24, dtype=np.float64) * ROWS)


class Net:
    def __init__(self, send, recv, core_send, core_recv, sibling):
        self.send, self.recv, self.core_send, self.core_recv = send, recv, core_send, core_recv
        self.sibling = sibling
        self.count = 0
        self.sent = []

    def describe(self, region, i, peer):
        ref = region()
        return pltpu.make_async_remote_copy(
            src_ref=ref, dst_ref=ref, send_sem=self.send.at[i], recv_sem=self.recv.at[i],
            device_id=peer, device_id_type=pl.DeviceIdType.MESH)

    def put(self, region, peer):
        i = self.count
        self.count += 1
        self.describe(region, i, peer).start()
        self.sent.append((region, i, peer))
        return i

    def got(self, region, i):
        self.describe(region, i, self.sibling).wait_recv()

    def core(self, region, k):
        ref = region()
        return pltpu.make_async_remote_copy(
            src_ref=ref, dst_ref=ref, send_sem=self.core_send.at[k], recv_sem=self.core_recv.at[k],
            device_id=self.sibling, device_id_type=pl.DeviceIdType.MESH)

    def finish(self):
        for region, i, peer in self.sent:
            self.describe(region, i, peer).wait_send()


def ring(net, reg, half, plus, minus, here, before, after, across, core):
    ids = {}

    def first():
        ids["p"] = net.put(lambda: reg(here), plus)
        ids["m"] = net.put(lambda: reg(here), minus)

    def second():
        net.got(lambda: reg(before), ids["p"])
        net.got(lambda: reg(after), ids["m"])
        ids["pp"] = net.put(lambda: half(before, 0), plus)
        ids["mm"] = net.put(lambda: half(after, 1), minus)
        core(lambda: reg(before))
        core(lambda: reg(after))

    def third():
        net.got(lambda: half(across, 0), ids["pp"])
        net.got(lambda: half(across, 1), ids["mm"])
        core(lambda: reg(across))

    return [first, second, third]


def chain(*rings):
    steps = list(rings[0])
    for following in rings[1:]:
        last = steps.pop()

        def joined(last=last, start=following[0]):
            last()
            start()

        steps.append(joined)
        steps.extend(following[1:])
    return steps


def beside(*lists):
    def step(k):
        def run():
            for steps in lists:
                steps[k]()
        return run
    return [step(k) for k in range(len(lists[0]))]


def kernel(lengths, resp, prompt, gain, wq, wk, wv, q_bias, k_bias, v_bias, wo, cos_b, sin_b, cos_a, sin_a,
           resid_out, squares,
           x_resp, x_prompt, wq_all, wkv_all, wo_one, wo_two, kv_all, kv_own, q_all, attended, acc,
           send, recv, core_send, core_recv, att_send, att_recv, local, out_sem):
    g, s, t = lax.axis_index("group"), lax.axis_index("sample"), lax.axis_index("tensor")
    z, xh, c = s // 4, lax.rem(s // 2, 2), lax.rem(s, 2)
    x = 2 * xh + g

    def wrap(v):
        return lax.rem(v + 4, 4)

    def place(zz, xx, cc, tt):
        return (lax.rem(xx, 2), zz * 4 + (xx // 2) * 2 + cc, tt)

    zm, zp, z2 = wrap(z - 1), wrap(z + 1), wrap(z + 2)
    xm, xp, x2 = wrap(x - 1), wrap(x + 1), wrap(x + 2)
    tm, tp, t2 = wrap(t - 1), wrap(t + 1), wrap(t + 2)
    at_zp, at_zm = place(zp, x, c, t), place(zm, x, c, t)
    at_xp, at_xm, at_x2 = place(z, xp, c, t), place(z, xm, c, t), place(z, x2, c, t)
    at_tp, at_tm = place(z, x, c, tp), place(z, x, c, tm)
    sibling = place(z, x, 1 - c, t)
    other = 1 - xh

    part = pl.ds(pl.multiple_of(g * 160, 160), 160)
    part_one = pl.ds(pl.multiple_of(g * 160, 160), 80)
    part_two = pl.ds(pl.multiple_of(g * 160 + 80, 80), 80)
    loads = [
        pltpu.make_async_copy(wk.at[part], wkv_all.at[c, z, xh, g, :, pl.ds(0, 128)], local.at[0]),
        pltpu.make_async_copy(wv.at[part], wkv_all.at[c, z, xh, g, :, pl.ds(128, 128)], local.at[1]),
        pltpu.make_async_copy(wq.at[part], wq_all.at[c, z, xh, g], local.at[2]),
        pltpu.make_async_copy(wo.at[part_one], wo_one.at[c, t, z, xh, g], local.at[3]),
        pltpu.make_async_copy(wo.at[part_two], wo_two.at[c, z, xh, g, t], local.at[4]),
        pltpu.make_async_copy(prompt, x_prompt, local.at[5]),
        pltpu.make_async_copy(resp, x_resp, local.at[6]),
    ]
    for load in loads:
        load.start()

    barrier = pltpu.get_barrier_semaphore()
    for peer in (at_zp, at_zm, at_xp, at_xm, at_x2, at_tp, at_tm, sibling):
        pl.semaphore_signal(barrier, inc=1, device_id=peer, device_id_type=pl.DeviceIdType.MESH)
    pl.semaphore_wait(barrier, 8)

    net = Net(send, recv, core_send, core_recv, sibling)

    def to_core(k):
        return lambda region: net.core(region, k).start()

    def rows_half(r0, count, which):
        low = (count // 2 + 15) // 16 * 16
        return pl.ds(r0, low) if which == 0 else pl.ds(r0 + low, count - low)

    def plane(reg, split_a, split_b, core):
        (ra, na, ca), (rb, nb, cb) = split_a, split_b
        da, db = pl.ds(ra, na), pl.ds(rb, nb)
        where = {"m": (xm // 2, lax.rem(xm, 2)), "p": (xp // 2, lax.rem(xp, 2)), "h": (xh, g), "2": (x2 // 2, lax.rem(x2, 2))}
        a1 = ring(net, lambda p: reg(p, xh, g, da, ca), lambda p, w: reg(p, xh, g, rows_half(ra, na, w), ca),
                  at_zp, at_zm, z, zm, zp, z2, core)
        a2 = ring(net, lambda p: reg(ALL, *where[p], da, ca), lambda p, w: reg(pl.ds(2 * w, 2), *where[p], da, ca),
                  at_xp, at_xm, "h", "m", "p", "2", core)
        b1 = ring(net, lambda p: reg(z, *where[p], db, cb), lambda p, w: reg(z, *where[p], rows_half(rb, nb, w), cb),
                  at_xp, at_xm, "h", "m", "p", "2", core)
        b2 = ring(net, lambda p: reg(p, ALL, ALL, db, cb), lambda p, w: reg(p, pl.ds(w, 1), ALL, db, cb),
                  at_zp, at_zm, z, zm, zp, z2, core)
        steps = beside(chain(a1, a2), chain(b1, b2))
        start = steps[0]

        def first():
            start()
            core(lambda: reg(z, xh, g, ALL, ALL))

        steps[0] = first
        return steps

    wkv_steps = plane(lambda zz, hh, gg, r, k: wkv_all.at[c, zz, hh, gg, r, k],
                      (0, 160, pl.ds(0, 128)), (0, 160, pl.ds(128, 128)), to_core(0))
    wq_steps = plane(lambda zz, hh, gg, r, k: wq_all.at[c, zz, hh, gg, r, k],
                     (0, 80, ALL), (80, 80, ALL), to_core(1))
    one_steps = chain(
        plane(lambda zz, hh, gg, r, k: wo_one.at[c, t, zz, hh, gg, r, k],
              (0, 80, pl.ds(0, 384)), (0, 80, pl.ds(384, 256)), to_core(2)),
        ring(net, lambda p: wo_one.at[c, p], lambda p, w: wo_one.at[c, p, pl.ds(2 * w, 2)],
             at_tp, at_tm, t, tm, tp, t2, to_core(2)))
    two_steps = chain(
        ring(net, lambda p: wo_two.at[c, z, xh, g, p],
             lambda p, w: wo_two.at[c, z, xh, g, p, rows_half(0, 80, w)],
             at_tp, at_tm, t, tm, tp, t2, lambda region: None),
        plane(lambda zz, hh, gg, r, k: wo_two.at[c, zz, hh, gg, :, r, k],
              (0, 80, pl.ds(0, 256)), (0, 80, pl.ds(256, 384)), to_core(3)))

    ka, kb = pl.ds(0, 224), pl.ds(224, 288)
    kv_core = to_core(4)
    kv_ids = {}
    kv_za = ring(net, lambda p: kv_all.at[c, p, xh, ka], lambda p, w: kv_all.at[c, p, xh, pl.ds(112 * w, 112)],
                 at_zp, at_zm, z, zm, zp, z2, kv_core)
    kv_zb = ring(net, lambda p: kv_all.at[c, p, :, kb], lambda p, w: kv_all.at[c, p, pl.ds(w, 1), kb],
                 at_zp, at_zm, z, zm, zp, z2, kv_core)

    def kv_0():
        kv_za[0]()
        kv_ids["b"] = net.put(lambda: kv_all.at[c, z, xh, kb], at_x2)
        kv_core(lambda: kv_all.at[c, z, xh])

    def kv_1():
        kv_za[1]()
        net.got(lambda: kv_all.at[c, z, other, kb], kv_ids["b"])
        kv_core(lambda: kv_all.at[c, z, other, kb])
        kv_zb[0]()

    def kv_2():
        kv_za[2]()
        kv_ids["a"] = net.put(lambda: kv_all.at[c, :, xh, ka], at_x2)
        kv_zb[1]()

    def kv_3():
        net.got(lambda: kv_all.at[c, :, other, ka], kv_ids["a"])
        kv_core(lambda: kv_all.at[c, :, other, ka])
        kv_zb[2]()

    def core_in(k, buf):
        net.core(lambda: buf.at[1 - c], k).wait_recv()

    gain_row = gain[...].astype(F32)

    def normalize(ref):
        def rows16(i, _):
            r = pl.ds(pl.multiple_of(i * 16, 16), 16)
            v = ref[r, :].astype(F32)
            scale = lax.rsqrt(jnp.mean(v * v, axis=-1, keepdims=True) + EPS)
            ref[r, :] = (v * scale * gain_row).astype(BF16)
            return 0
        lax.fori_loop(0, ROWS // 16, rows16, 0)

    def project(rows_ref, weights, width):
        acc[:, :width] = jnp.zeros((ROWS, width), F32)

        def block(i, _):
            left = rows_ref[:, pl.ds(pl.multiple_of(i * 640, 640), 640)]
            zz, hh = i // 2, lax.rem(i, 2)
            right = jnp.concatenate(
                [weights[0, zz, hh].reshape(320, width), weights[1, zz, hh].reshape(320, width)], 0)
            acc[:, :width] += jnp.dot(left, right, preferred_element_type=F32)
            return 0
        lax.fori_loop(0, 8, block, 0)

    def angles(block):
        ca, sa = cos_a[pl.ds(block, 1), :], sin_a[pl.ds(block, 1), :]
        cb, sb = cos_b[...], sin_b[...]
        lane = lax.broadcasted_iota(jnp.int32, (ROWS, HEAD), 1)
        sine = sa * cb + ca * sb
        return ca * cb - sa * sb, jnp.where(lane < HEAD // 2, -sine, sine)

    def rope(u, cosine, sine):
        return u * cosine + pltpu.roll(u, HEAD // 2, 1) * sine

    def keys_values(block):
        cosine, sine = angles(block)
        keys = rope(acc[:, 0:128] + k_bias[...].astype(F32), cosine, sine).astype(BF16)
        return keys, (acc[:, 128:256] + v_bias[...].astype(F32)).astype(BF16)

    loads[0].wait()
    loads[1].wait()
    wkv_steps[0]()
    loads[2].wait()
    loads[3].wait()
    loads[4].wait()
    two_steps[0]()
    wq_steps[0]()
    loads[5].wait()
    normalize(x_prompt)
    wkv_steps[1]()
    two_steps[1]()
    wkv_steps[2]()
    one_steps[0]()
    wq_steps[1]()
    wkv_steps[3]()
    loads[6].wait()
    normalize(x_resp)
    wkv_steps[4]()
    one_steps[1]()
    wq_steps[2]()
    core_in(0, wkv_all)
    project(x_prompt, wkv_all, 256)
    keys, values = keys_values(s)
    kv_all[c, z, xh, :, 0:128] = keys
    kv_all[c, z, xh, :, 128:256] = values
    kv_0()
    one_steps[2]()
    project(x_resp, wkv_all, 256)
    keys, values = keys_values(16)
    kv_own[:, 0:128] = keys
    kv_own[:, 128:256] = values
    wq_steps[3]()
    kv_1()
    one_steps[3]()
    kv_2()
    wq_steps[4]()
    one_steps[4]()
    core_in(1, wq_all)
    project(x_resp, wq_all, Q_COLS)
    cosine, sine = angles(16)
    for h in range(Q_HEADS):
        cols = slice(h * HEAD, (h + 1) * HEAD)
        q = rope(acc[:, cols] + q_bias[:, cols].astype(F32), cosine, sine)
        q_all[h] = (q * (math.log2(math.e) / math.sqrt(HEAD))).astype(BF16)
    reload = pltpu.make_async_copy(resp, x_resp, local.at[7])
    reload.start()
    kv_3()
    two_steps[2]()
    core_in(4, kv_all)

    length = lengths[0]

    def att_copy(h, k, region, peer):
        return pltpu.make_async_remote_copy(
            src_ref=region, dst_ref=region, send_sem=att_send.at[h, k], recv_sem=att_recv.at[h, k],
            device_id=peer, device_id_type=pl.DeviceIdType.MESH)

    def att_first(h):
        att_copy(h, 0, attended.at[t, h], at_tp).start()
        att_copy(h, 1, attended.at[t, h], at_tm).start()

    def att_second(h):
        att_copy(h, 0, attended.at[tm, h], at_tp).wait_recv()
        att_copy(h, 1, attended.at[tp, h], at_tm).wait_recv()
        att_copy(h, 2, attended.at[tm, h, pl.ds(0, 256)], at_tp).start()
        att_copy(h, 3, attended.at[tp, h, pl.ds(256, 256)], at_tm).start()

    def att_third(h):
        att_copy(h, 2, attended.at[t2, h, pl.ds(0, 256)], at_tp).wait_recv()
        att_copy(h, 3, attended.at[t2, h, pl.ds(256, 256)], at_tm).wait_recv()

    def att_sent(h):
        att_copy(h, 0, attended.at[t, h], at_tp).wait_send()
        att_copy(h, 1, attended.at[t, h], at_tm).wait_send()
        att_copy(h, 2, attended.at[tm, h, pl.ds(0, 256)], at_tp).wait_send()
        att_copy(h, 3, attended.at[tp, h, pl.ds(256, 256)], at_tm).wait_send()

    def head(h, _):
        q = q_all[h]

        def scores(j):
            k = kv_all[j // 2, pl.ds(2 * (j % 2), 2), :, :, 0:128].reshape(2048, HEAD)
            return lax.dot_general(q, k, NT, preferred_element_type=F32)

        def widened(v):
            return jnp.concatenate([v, jnp.ones_like(v)], 1)

        score = lax.dot_general(q, kv_own[:, 0:128], NT, preferred_element_type=F32)
        row = lax.broadcasted_iota(jnp.int32, (ROWS, ROWS), 0)
        col = lax.broadcasted_iota(jnp.int32, (ROWS, ROWS), 1)
        score = jnp.where(col <= row, score, -1e30)
        value = widened(kv_own[:, 128:256])
        highest = total = None
        for j in range(5):
            if j < 4:
                score_next = scores(j)
                value_next = widened(kv_all[j // 2, pl.ds(2 * (j % 2), 2), :, :, 128:256].reshape(2048, HEAD))
            top = jnp.max(score, axis=1, keepdims=True)
            fresh = top if j == 0 else jnp.maximum(highest, top)
            probs = jnp.exp2(score - fresh).astype(BF16)
            term = jnp.dot(probs, value, preferred_element_type=F32)
            total = term if j == 0 else total * jnp.exp2(highest - fresh) + term
            highest = fresh
            score, value = score_next, value_next
        live = lax.broadcasted_iota(jnp.int32, (ROWS, HEAD), 0) < length
        attended[t, h] = jnp.where(live, total[:, :HEAD] / total[:, HEAD:], 0.0).astype(BF16)
        att_first(h)

        @pl.when(h > 0)
        def _():
            att_second(h - 1)

        @pl.when(h == 0)
        def _():
            two_steps[3]()

        @pl.when(h == 1)
        def _():
            two_steps[4]()

        @pl.when(h == 2)
        def _():
            one_steps[5]()

        @pl.when(h == 3)
        def _():
            two_steps[5]()
        return 0

    lax.fori_loop(0, Q_HEADS, head, 0)
    att_second(Q_HEADS - 1)
    one_steps[6]()
    two_steps[6]()
    for h in range(Q_HEADS):
        att_third(h)
    core_in(2, wo_one)
    core_in(3, wo_two)
    reload.wait()

    squares[...] = jnp.zeros((ROWS, 128), F32)

    def out_copy(i):
        cols = pl.ds(pl.multiple_of(i * 640, 640), 640)
        return pltpu.make_async_copy(x_prompt.at[:, cols], resid_out.at[:, cols], out_sem.at[i])

    def block(i, _):
        zz, hh = i // 2, lax.rem(i, 2)
        cols = pl.ds(pl.multiple_of(i * 640, 640), 640)
        total = x_resp[:, cols].astype(F32)
        for tt in range(4):
            left = jnp.concatenate([attended[tt, h] for h in range(Q_HEADS)], 1)
            right = jnp.concatenate(
                [buf for cc in range(2) for gg in range(2)
                 for buf in (wo_one[cc, tt, zz, hh, gg], wo_two[cc, zz, hh, gg, tt])], 0)
            total = total + lax.dot_general(left, right, NT, preferred_element_type=F32)
        x_prompt[:, cols] = total.astype(BF16)
        square = total * total
        squares[...] += sum(square[:, k * 128:(k + 1) * 128] for k in range(5))
        out_copy(i).start()
        return 0

    lax.fori_loop(0, 8, block, 0)

    net.finish()
    for k, buf in enumerate((wkv_all, wq_all, wo_one, wo_two, kv_all)):
        net.core(lambda: buf.at[c], k).wait_send()
    for h in range(Q_HEADS):
        att_sent(h)
    for i in range(8):
        out_copy(i).wait()


def on_device(resp_hidden, prompt_hidden, lengths, norm_gain, wq, wk, wv, q_bias, k_bias, value_bias, wo_t, post_gain):
    resp = resp_hidden[0]
    tables = [jnp.asarray(a) for a in rope_tables()]
    vmem = pl.BlockSpec(memory_space=pltpu.VMEM)
    hbm = pl.BlockSpec(memory_space=pl.ANY)
    smem = pl.BlockSpec(memory_space=pltpu.SMEM)
    dma = pltpu.SemaphoreType.DMA
    resid, squares = pl.pallas_call(
        kernel,
        out_shape=(jax.ShapeDtypeStruct((ROWS, WIDTH), BF16), jax.ShapeDtypeStruct((ROWS, 128), F32)),
        in_specs=[smem, hbm, hbm, vmem, hbm, hbm, hbm, vmem, vmem, vmem, hbm, vmem, vmem, vmem, vmem],
        out_specs=(hbm, vmem),
        scratch_shapes=[
            pltpu.VMEM((ROWS, WIDTH), BF16),
            pltpu.VMEM((ROWS, WIDTH), BF16),
            pltpu.VMEM((2, 4, 2, 2, 160, Q_COLS), BF16),
            pltpu.VMEM((2, 4, 2, 2, 160, 256), BF16),
            pltpu.VMEM((2, 4, 4, 2, 2, 80, Q_COLS), BF16),
            pltpu.VMEM((2, 4, 2, 2, 4, 80, Q_COLS), BF16),
            pltpu.VMEM((2, 4, 2, ROWS, 256), BF16),
            pltpu.VMEM((ROWS, 256), BF16),
            pltpu.VMEM((Q_HEADS, ROWS, HEAD), BF16),
            pltpu.VMEM((4, Q_HEADS, ROWS, HEAD), BF16),
            pltpu.VMEM((ROWS, Q_COLS), F32),
            dma((90,)), dma((90,)), dma((5,)), dma((5,)), dma((Q_HEADS, 4)), dma((Q_HEADS, 4)), dma((8,)), dma((8,)),
        ],
        compiler_params=pltpu.CompilerParams(
            collective_id=0, has_side_effects=True, vmem_limit_bytes=67000000),
        cost_estimate=pl.CostEstimate(flops=31_000_000_000, bytes_accessed=30_000_000, transcendentals=22_000_000),
    )(lengths, resp, prompt_hidden, norm_gain[None], wq, wk, wv, q_bias[None], k_bias[None], value_bias[None], wo_t,
      *tables)
    meansq = jnp.sum(squares, axis=-1, keepdims=True) / WIDTH
    live = (jnp.arange(ROWS) < lengths[0])[:, None]
    mixed = resid.astype(F32) * lax.rsqrt(meansq + EPS) * post_gain.astype(F32)
    return jnp.where(live, mixed, 0.0).astype(BF16)[None]


def solution(mesh):
    placed = (
        P(("group", "sample"), None, None),
        P(("group", "sample"), None),
        P(("group", "sample")),
        P(),
        P("sample", "tensor"),
        P("sample", "tensor"),
        P("sample", "tensor"),
        P("tensor"),
        P("tensor"),
        P("tensor"),
        P("sample", "tensor"),
        P(),
    )
    return jax.shard_map(
        on_device,
        mesh=mesh,
        in_specs=placed,
        out_specs=P(("group", "sample"), None, None),
        check_vma=False,
    )
```

```python
import math

import jax
import jax.numpy as jnp
import numpy as np
from jax import lax
from jax.experimental import pallas as pl
from jax.experimental.pallas import tpu as pltpu
from jax.sharding import PartitionSpec as P

HEAD = 128
EPS = 1e-06
THETA = 1000000.0
WIDTH = 5120
ROWS = 512
Q_HEADS = 5
Q_COLS = Q_HEADS * HEAD
F32 = jnp.float32
BF16 = jnp.bfloat16
NT = (((1,), (1,)), ((), ()))
ALL = slice(None)
ONE = 64
TWO = 160 - ONE


def rope_tables():
    half = np.arange(HEAD // 2, dtype=np.float64)
    inverse = THETA ** (-2.0 * half / HEAD)

    def pair(positions):
        angle = positions[:, None] * inverse[None, :]
        cosine, sine = np.cos(angle), np.sin(angle)
        both = np.concatenate([cosine, cosine], 1), np.concatenate([sine, sine], 1)
        return both[0].astype(np.float32), both[1].astype(np.float32)

    return pair(np.arange(ROWS, dtype=np.float64)) + pair(np.arange(24, dtype=np.float64) * ROWS)


class Net:
    def __init__(self, send, recv, core_send, core_recv, sibling, c):
        self.send, self.recv, self.core_send, self.core_recv = send, recv, core_send, core_recv
        self.sibling = sibling
        self.c = self.who = c
        self.count = 0
        self.sent = []
        self.shared = []

    def describe(self, region, i, peer):
        ref = region()
        return pltpu.make_async_remote_copy(
            src_ref=ref, dst_ref=ref, send_sem=self.send.at[i], recv_sem=self.recv.at[i],
            device_id=peer, device_id_type=pl.DeviceIdType.MESH)

    def put(self, region, peer):
        i = self.count
        self.count += 1
        self.describe(region, i, peer).start()
        self.sent.append((region, i, peer))
        return i

    def got(self, region, i):
        self.describe(region, i, self.sibling).wait_recv()

    def describe_core(self, region, i):
        ref = region()
        return pltpu.make_async_remote_copy(
            src_ref=ref, dst_ref=ref, send_sem=self.core_send.at[i], recv_sem=self.core_recv.at[i],
            device_id=self.sibling, device_id_type=pl.DeviceIdType.MESH)

    def core(self, region, group):
        i = len(self.shared)
        self.describe_core(region, i).start()
        self.shared.append((region, group))

    def core_in(self, group):
        self.who = 1 - self.c
        for i, (region, belongs) in enumerate(self.shared):
            if belongs == group:
                self.describe_core(region, i).wait_recv()
        self.who = self.c

    def finish(self):
        for region, i, peer in self.sent:
            self.describe(region, i, peer).wait_send()
        for i, (region, _) in enumerate(self.shared):
            self.describe_core(region, i).wait_send()


def ring(net, reg, half, plus, minus, here, before, after, across, core, core_last=None):
    ids = {}

    def first():
        ids["p"] = net.put(lambda: reg(here), plus)
        ids["m"] = net.put(lambda: reg(here), minus)

    def second():
        net.got(lambda: reg(before), ids["p"])
        net.got(lambda: reg(after), ids["m"])
        ids["pp"] = net.put(lambda: half(before, 0), plus)
        ids["mm"] = net.put(lambda: half(after, 1), minus)
        core(lambda: reg(before))
        core(lambda: reg(after))

    def third():
        net.got(lambda: half(across, 0), ids["pp"])
        net.got(lambda: half(across, 1), ids["mm"])
        (core_last or core)(lambda: reg(across))

    return [first, second, third]


def direct(net, reg, plus, minus, far, here, before, after, across, core):
    ids = {}

    def first():
        ids["p"] = net.put(lambda: reg(here), plus)
        ids["m"] = net.put(lambda: reg(here), minus)
        ids["f"] = net.put(lambda: reg(here), far)

    def second():
        net.got(lambda: reg(before), ids["p"])
        net.got(lambda: reg(after), ids["m"])
        core(lambda: reg(before))
        core(lambda: reg(after))
        net.got(lambda: reg(across), ids["f"])
        core(lambda: reg(across))

    return [first, second]


def chain(*rings):
    steps = list(rings[0])
    for following in rings[1:]:
        last = steps.pop()

        def joined(last=last, start=following[0]):
            last()
            start()

        steps.append(joined)
        steps.extend(following[1:])
    return steps


def beside(*lists):
    def step(k):
        def run():
            for steps in lists:
                steps[k]()
        return run
    return [step(k) for k in range(len(lists[0]))]


def kernel(lengths, resp, prompt, gain, wq, wk, wv, q_bias, k_bias, v_bias, wo, cos_b, sin_b, cos_a, sin_a,
           resid_out,
           x_resp, x_prompt, wq_all, wkv_all, wo_one, wo_two, kv_all, kv_own, q_all, attended, acc,
           send, recv, core_send, core_recv, att_send, att_recv, local, out_sem):
    g, s, t = lax.axis_index("group"), lax.axis_index("sample"), lax.axis_index("tensor")
    z, xh, c = s // 4, lax.rem(s // 2, 2), lax.rem(s, 2)
    x = 2 * xh + g

    def wrap(v):
        return lax.rem(v + 4, 4)

    def place(zz, xx, cc, tt):
        return (lax.rem(xx, 2), zz * 4 + (xx // 2) * 2 + cc, tt)

    zm, zp, z2 = wrap(z - 1), wrap(z + 1), wrap(z + 2)
    xm, xp, x2 = wrap(x - 1), wrap(x + 1), wrap(x + 2)
    tm, tp, t2 = wrap(t - 1), wrap(t + 1), wrap(t + 2)
    at_zp, at_zm = place(zp, x, c, t), place(zm, x, c, t)
    at_xp, at_xm, at_x2 = place(z, xp, c, t), place(z, xm, c, t), place(z, x2, c, t)
    at_z2, at_t2 = place(z2, x, c, t), place(z, x, c, t2)
    at_tp, at_tm = place(z, x, c, tp), place(z, x, c, tm)
    sibling = place(z, x, 1 - c, t)
    other = 1 - xh

    part = pl.ds(pl.multiple_of(g * 160, 160), 160)
    part_one = pl.ds(pl.multiple_of(g * 160, 160), ONE)
    part_two = pl.ds(pl.multiple_of(g * 160 + ONE, 16), TWO)
    loads = [
        pltpu.make_async_copy(wk.at[part], wkv_all.at[c, z, xh, g, :, pl.ds(0, 128)], local.at[0]),
        pltpu.make_async_copy(wv.at[part], wkv_all.at[c, z, xh, g, :, pl.ds(128, 128)], local.at[1]),
        pltpu.make_async_copy(wq.at[part], wq_all.at[c, z, xh, g], local.at[2]),
        pltpu.make_async_copy(wo.at[part_one], wo_one.at[c, t, z, xh, g], local.at[3]),
        pltpu.make_async_copy(wo.at[part_two], wo_two.at[c, z, xh, g, t], local.at[4]),
        pltpu.make_async_copy(prompt, x_prompt, local.at[5]),
        pltpu.make_async_copy(resp, x_resp, local.at[6]),
    ]
    for load in loads:
        load.start()

    barrier = pltpu.get_barrier_semaphore()
    for peer in (at_zp, at_zm, at_z2, at_t2, at_xp, at_xm, at_x2, at_tp, at_tm, sibling):
        pl.semaphore_signal(barrier, inc=1, device_id=peer, device_id_type=pl.DeviceIdType.MESH)
    pl.semaphore_wait(barrier, 10)

    net = Net(send, recv, core_send, core_recv, sibling, c)

    def to_core(k):
        return lambda region: net.core(region, k)

    def rows_half(r0, count, which):
        low = (count // 2 + 15) // 16 * 16
        return pl.ds(r0, low) if which == 0 else pl.ds(r0 + low, count - low)

    def plane(reg, split_a, split_b, core, core_last=None, straight=(False, False)):
        (ra, na, ca), (rb, nb, cb) = split_a, split_b
        da, db = pl.ds(ra, na), pl.ds(rb, nb)
        where = {"m": (xm // 2, lax.rem(xm, 2)), "p": (xp // 2, lax.rem(xp, 2)), "h": (xh, g), "2": (x2 // 2, lax.rem(x2, 2))}

        def gather(stage, whole, half, axis):
            plus, minus, far, places = (at_zp, at_zm, at_z2, (z, zm, zp, z2)) if axis == "z" else (
                at_xp, at_xm, at_x2, ("h", "m", "p", "2"))
            if straight[stage]:
                return direct(net, whole, plus, minus, far, *places, core)
            return ring(net, whole, half, plus, minus, *places, core, core_last if stage else None)

        a1 = gather(0, lambda p: reg(p, xh, g, da, ca), lambda p, w: reg(p, xh, g, rows_half(ra, na, w), ca), "z")
        a2 = gather(1, lambda p: reg(ALL, *where[p], da, ca), lambda p, w: reg(pl.ds(2 * w, 2), *where[p], da, ca), "x")
        b1 = gather(0, lambda p: reg(z, *where[p], db, cb), lambda p, w: reg(z, *where[p], rows_half(rb, nb, w), cb), "x")
        b2 = gather(1, lambda p: reg(p, ALL, ALL, db, cb), lambda p, w: reg(p, pl.ds(w, 1), ALL, db, cb), "z")
        steps = beside(chain(a1, a2), chain(b1, b2))
        start = steps[0]

        def first():
            start()
            core(lambda: reg(z, xh, g, ALL, ALL))

        steps[0] = first
        return steps

    wkv_steps = plane(lambda zz, hh, gg, r, k: wkv_all.at[net.who, zz, hh, gg, r, k],
                      (0, 160, pl.ds(0, 128)), (0, 160, pl.ds(128, 128)), to_core(0))
    wq_steps = plane(lambda zz, hh, gg, r, k: wq_all.at[net.who, zz, hh, gg, r, k],
                     (0, 80, ALL), (80, 80, ALL), to_core(1))
    one_steps = chain(
        plane(lambda zz, hh, gg, r, k: wo_one.at[net.who, t, zz, hh, gg, r, k],
              (0, ONE, pl.ds(0, 384)), (0, ONE, pl.ds(384, 256)), to_core(2)),
        ring(net, lambda p: wo_one.at[net.who, p], lambda p, w: wo_one.at[net.who, p, pl.ds(2 * w, 2)],
             at_tp, at_tm, t, tm, tp, t2, to_core(2)))
    two_steps = chain(
        ring(net, lambda p: wo_two.at[net.who, z, xh, g, p],
             lambda p, w: wo_two.at[net.who, z, xh, g, p, rows_half(0, TWO, w)],
             at_tp, at_tm, t, tm, tp, t2, lambda region: None),
        plane(lambda zz, hh, gg, r, k: wo_two.at[net.who, zz, hh, gg, :, r, k],
              (0, TWO, pl.ds(0, 256)), (0, TWO, pl.ds(256, 384)), to_core(3), to_core(5)))

    ka, kb = pl.ds(0, 224), pl.ds(224, 288)
    kv_core = to_core(4)
    kv_ids = {}
    kv_za = ring(net, lambda p: kv_all.at[net.who, p, xh, ka], lambda p, w: kv_all.at[net.who, p, xh, pl.ds(112 * w, 112)],
                 at_zp, at_zm, z, zm, zp, z2, kv_core)
    kv_zb = ring(net, lambda p: kv_all.at[net.who, p, :, kb], lambda p, w: kv_all.at[net.who, p, pl.ds(w, 1), kb],
                 at_zp, at_zm, z, zm, zp, z2, kv_core)

    def kv_0():
        kv_za[0]()
        kv_ids["b"] = net.put(lambda: kv_all.at[net.who, z, xh, kb], at_x2)
        kv_core(lambda: kv_all.at[net.who, z, xh])

    def kv_1():
        kv_za[1]()
        net.got(lambda: kv_all.at[net.who, z, other, kb], kv_ids["b"])
        kv_core(lambda: kv_all.at[net.who, z, other, kb])
        kv_zb[0]()

    def kv_2():
        kv_za[2]()
        kv_ids["a"] = net.put(lambda: kv_all.at[net.who, :, xh, ka], at_x2)
        kv_zb[1]()

    def kv_3():
        net.got(lambda: kv_all.at[net.who, :, other, ka], kv_ids["a"])
        kv_core(lambda: kv_all.at[net.who, :, other, ka])
        kv_zb[2]()

    gain_row = gain[...].astype(F32).reshape(1, WIDTH)
    q_row = q_bias[...].astype(F32).reshape(1, Q_COLS)
    k_row = k_bias[...].astype(F32).reshape(1, HEAD)
    v_row = v_bias[...].astype(F32).reshape(1, HEAD)

    def normalize(ref, first, count):
        def rows32(i, _):
            r = pl.ds(pl.multiple_of(first + i * 32, 32), 32)
            v = ref[r, :].astype(F32)
            scale = lax.rsqrt(jnp.mean(v * v, axis=-1, keepdims=True) + EPS)
            ref[r, :] = (v * scale * gain_row).astype(BF16)
            return 0
        lax.fori_loop(0, count // 32, rows32, 0)

    def project(rows_ref, weights, width):
        acc[:, :width] = jnp.zeros((ROWS, width), F32)

        def block(zz, _):
            left = rows_ref[:, pl.ds(pl.multiple_of(zz * 1280, 1280), 1280)]
            right = jnp.concatenate(
                [weights[cc, zz, hh].reshape(320, width) for hh in range(2) for cc in range(2)], 0)
            acc[:, :width] += jnp.dot(left, right, preferred_element_type=F32)
            return 0
        lax.fori_loop(0, 4, block, 0)

    def angles(block):
        ca, sa = cos_a[pl.ds(block, 1), :], sin_a[pl.ds(block, 1), :]
        cb, sb = cos_b[...], sin_b[...]
        lane = lax.broadcasted_iota(jnp.int32, (ROWS, HEAD), 1)
        sine = sa * cb + ca * sb
        return ca * cb - sa * sb, jnp.where(lane < HEAD // 2, -sine, sine)

    def rope(u, cosine, sine):
        return u * cosine + pltpu.roll(u, HEAD // 2, 1) * sine

    def keys_values(block):
        cosine, sine = angles(block)
        keys = rope(acc[:, 0:128] + k_row, cosine, sine).astype(BF16)
        return keys, (acc[:, 128:256] + v_row).astype(BF16)

    loads[3].wait()
    one_steps[0]()
    loads[4].wait()
    two_steps[0]()
    loads[2].wait()
    wq_steps[0]()
    loads[0].wait()
    loads[1].wait()
    wkv_steps[0]()
    one_steps[1]()
    wq_steps[1]()
    wkv_steps[1]()
    one_steps[2]()
    two_steps[1]()
    loads[5].wait()
    normalize(x_prompt, 0, 256)
    wkv_steps[2]()
    normalize(x_prompt, 256, 256)
    one_steps[3]()
    wkv_steps[3]()
    wq_steps[2]()
    loads[6].wait()
    normalize(x_resp, 0, 256)
    one_steps[4]()
    normalize(x_resp, 256, 256)
    wkv_steps[4]()
    net.core_in(0)
    project(x_prompt, wkv_all, 256)
    keys, values = keys_values(s)
    kv_all[c, z, xh, :, 0:128] = keys
    kv_all[c, z, xh, :, 128:256] = values
    kv_0()
    two_steps[2]()
    kv_1()
    wq_steps[3]()
    two_steps[3]()
    project(x_resp, wkv_all, 256)
    keys, values = keys_values(16)
    kv_own[:, 0:128] = keys
    kv_own[:, 128:256] = values
    kv_2()
    wq_steps[4]()
    one_steps[5]()
    two_steps[4]()
    net.core_in(1)
    project(x_resp, wq_all, Q_COLS)
    cosine, sine = angles(16)
    for h in range(Q_HEADS):
        cols = slice(h * HEAD, (h + 1) * HEAD)
        q = rope(acc[:, cols] + q_row[:, cols], cosine, sine)
        q_all[h] = (q * (math.log2(math.e) / math.sqrt(HEAD))).astype(BF16)
    reload = pltpu.make_async_copy(resp, x_resp, local.at[7])
    reload.start()
    kv_3()
    net.core_in(4)

    length = lengths[0]

    def att_copy(h, k, region, peer):
        return pltpu.make_async_remote_copy(
            src_ref=region, dst_ref=region, send_sem=att_send.at[h, k], recv_sem=att_recv.at[h, k],
            device_id=peer, device_id_type=pl.DeviceIdType.MESH)

    def att_first(h):
        att_copy(h, 0, attended.at[t, h], at_tp).start()
        att_copy(h, 1, attended.at[t, h], at_tm).start()

    def att_second(h):
        att_copy(h, 0, attended.at[tm, h], at_tp).wait_recv()
        att_copy(h, 1, attended.at[tp, h], at_tm).wait_recv()
        att_copy(h, 2, attended.at[tm, h, pl.ds(0, 256)], at_tp).start()
        att_copy(h, 3, attended.at[tp, h, pl.ds(256, 256)], at_tm).start()

    def att_third(h):
        att_copy(h, 2, attended.at[t2, h, pl.ds(0, 256)], at_tp).wait_recv()
        att_copy(h, 3, attended.at[t2, h, pl.ds(256, 256)], at_tm).wait_recv()

    def att_sent(h):
        att_copy(h, 0, attended.at[t, h], at_tp).wait_send()
        att_copy(h, 1, attended.at[t, h], at_tm).wait_send()
        att_copy(h, 2, attended.at[tm, h, pl.ds(0, 256)], at_tp).wait_send()
        att_copy(h, 3, attended.at[tp, h, pl.ds(256, 256)], at_tm).wait_send()

    def head(h, _):
        q = q_all[h]

        def scores(j):
            k = kv_all[j // 2, pl.ds(2 * (j % 2), 2), :, :, 0:128].reshape(2048, HEAD)
            return lax.dot_general(q, k, NT, preferred_element_type=F32)

        def widened(v):
            return jnp.concatenate([v, jnp.ones_like(v)], 1)

        score = lax.dot_general(q, kv_own[:, 0:128], NT, preferred_element_type=F32)
        row = lax.broadcasted_iota(jnp.int32, (ROWS, ROWS), 0)
        col = lax.broadcasted_iota(jnp.int32, (ROWS, ROWS), 1)
        score = jnp.where(col <= row, score, -1e30)
        value = widened(kv_own[:, 128:256])
        highest = total = None
        for j in range(5):
            if j < 4:
                score_next = scores(j)
                value_next = widened(kv_all[j // 2, pl.ds(2 * (j % 2), 2), :, :, 128:256].reshape(2048, HEAD))
            top = jnp.max(score, axis=1, keepdims=True)
            fresh = top if j == 0 else jnp.maximum(highest, top)
            probs = jnp.exp2(score - fresh).astype(BF16)
            term = jnp.dot(probs, value, preferred_element_type=F32)
            total = term if j == 0 else total * jnp.exp2(highest - fresh) + term
            highest = fresh
            score, value = score_next, value_next
        live = lax.broadcasted_iota(jnp.int32, (ROWS, HEAD), 0) < length
        attended[t, h] = jnp.where(live, total[:, :HEAD] / total[:, HEAD:], 0.0).astype(BF16)
        att_first(h)

        @pl.when(h > 0)
        def _():
            att_second(h - 1)

        @pl.when(h == 3)
        def _():
            two_steps[5]()
            one_steps[6]()

        @pl.when(h == 4)
        def _():
            net.core_in(2)
            net.core_in(3)
        return 0

    lax.fori_loop(0, Q_HEADS, head, 0)
    att_second(Q_HEADS - 1)
    reload.wait()
    for h in range(Q_HEADS):
        att_third(h)
    two_steps[6]()
    net.core_in(5)

    def out_copy(zz):
        cols = pl.ds(pl.multiple_of(zz * 1280, 1280), 1280)
        return pltpu.make_async_copy(x_prompt.at[:, cols], resid_out.at[:, cols], out_sem.at[zz])

    def block(zz, _):
        cols = pl.ds(pl.multiple_of(zz * 1280, 1280), 1280)
        left = jnp.concatenate([attended[tt, h] for tt in range(4) for h in range(Q_HEADS)], 1)
        right = jnp.concatenate(
            [jnp.concatenate(
                [buf for hh in range(2) for cc in range(2) for gg in range(2)
                 for buf in (wo_one[cc, tt, zz, hh, gg], wo_two[cc, zz, hh, gg, tt])], 0)
             for tt in range(4)], 1)
        branch = lax.dot_general(left, right, NT, preferred_element_type=F32)
        x_prompt[:, cols] = (x_resp[:, cols].astype(F32) + branch).astype(BF16)
        out_copy(zz).start()
        return 0

    lax.fori_loop(0, 4, block, 0)

    net.finish()
    for h in range(Q_HEADS):
        att_sent(h)
    for zz in range(4):
        out_copy(zz).wait()


def finish_kernel(lengths, resid, gain, mixed):
    rows = resid.shape[0]
    v = resid[...].astype(F32)
    scale = lax.rsqrt(jnp.mean(v * v, axis=-1, keepdims=True) + EPS)
    slot = pl.program_id(0) * rows + lax.broadcasted_iota(jnp.int32, (rows, 1), 0)
    out = v * scale * gain[...].astype(F32).reshape(1, WIDTH)
    mixed[...] = jnp.where(slot < lengths[0], out, 0.0).astype(BF16)


def on_device(resp_hidden, prompt_hidden, lengths, norm_gain, wq, wk, wv, q_bias, k_bias, value_bias, wo_t, post_gain):
    resp = resp_hidden[0]
    tables = [jnp.asarray(a) for a in rope_tables()]
    vmem = pl.BlockSpec(memory_space=pltpu.VMEM)
    hbm = pl.BlockSpec(memory_space=pl.ANY)
    smem = pl.BlockSpec(memory_space=pltpu.SMEM)
    dma = pltpu.SemaphoreType.DMA
    resid = pl.pallas_call(
        kernel,
        out_shape=jax.ShapeDtypeStruct((ROWS, WIDTH), BF16),
        in_specs=[smem, hbm, hbm, vmem, hbm, hbm, hbm, vmem, vmem, vmem, hbm, vmem, vmem, vmem, vmem],
        out_specs=hbm,
        scratch_shapes=[
            pltpu.VMEM((ROWS, WIDTH), BF16),
            pltpu.VMEM((ROWS, WIDTH), BF16),
            pltpu.VMEM((2, 4, 2, 2, 160, Q_COLS), BF16),
            pltpu.VMEM((2, 4, 2, 2, 160, 256), BF16),
            pltpu.VMEM((2, 4, 4, 2, 2, ONE, Q_COLS), BF16),
            pltpu.VMEM((2, 4, 2, 2, 4, TWO, Q_COLS), BF16),
            pltpu.VMEM((2, 4, 2, ROWS, 256), BF16),
            pltpu.VMEM((ROWS, 256), BF16),
            pltpu.VMEM((Q_HEADS, ROWS, HEAD), BF16),
            pltpu.VMEM((4, Q_HEADS, ROWS, HEAD), BF16),
            pltpu.VMEM((ROWS, Q_COLS), F32),
            dma((90,)), dma((90,)), dma((70,)), dma((70,)), dma((Q_HEADS, 4)), dma((Q_HEADS, 4)), dma((8,)), dma((8,)),
        ],
        compiler_params=pltpu.CompilerParams(
            collective_id=0, has_side_effects=True, vmem_limit_bytes=67000000),
        cost_estimate=pl.CostEstimate(flops=31_000_000_000, bytes_accessed=30_000_000, transcendentals=22_000_000),
    )(lengths, resp, prompt_hidden, norm_gain, wq, wk, wv, q_bias, k_bias, value_bias, wo_t,
      *tables)
    block = pl.BlockSpec((64, WIDTH), lambda i: (i, 0))
    mixed = pl.pallas_call(
        finish_kernel,
        out_shape=jax.ShapeDtypeStruct((ROWS, WIDTH), BF16),
        grid=(ROWS // 64,),
        in_specs=[smem, block, vmem],
        out_specs=block,
    )(lengths, resid, post_gain)
    return mixed[None]


def solution(mesh):
    placed = (
        P(("group", "sample"), None, None),
        P(("group", "sample"), None),
        P(("group", "sample")),
        P(),
        P("sample", "tensor"),
        P("sample", "tensor"),
        P("sample", "tensor"),
        P("tensor"),
        P("tensor"),
        P("tensor"),
        P("sample", "tensor"),
        P(),
    )
    return jax.shard_map(
        on_device,
        mesh=mesh,
        in_specs=placed,
        out_specs=P(("group", "sample"), None, None),
        check_vma=False,
    )
```

```python
import math

import jax
import jax.numpy as jnp
import numpy as np
from jax import lax
from jax.experimental import pallas as pl
from jax.experimental.pallas import tpu as pltpu
from jax.sharding import PartitionSpec as P

HEAD = 128
EPS = 1e-06
THETA = 1000000.0
WIDTH = 5120
ROWS = 512
Q_HEADS = 5
Q_COLS = Q_HEADS * HEAD
F32 = jnp.float32
BF16 = jnp.bfloat16
NT = (((1,), (1,)), ((), ()))
ALL = slice(None)
ONE, MID, TWO = 32, 48, 80


def rope_tables():
    half = np.arange(HEAD // 2, dtype=np.float64)
    inverse = THETA ** (-2.0 * half / HEAD)

    def pair(positions):
        angle = positions[:, None] * inverse[None, :]
        cosine, sine = np.cos(angle), np.sin(angle)
        both = np.concatenate([cosine, cosine], 1), np.concatenate([sine, sine], 1)
        return both[0].astype(np.float32), both[1].astype(np.float32)

    return pair(np.arange(ROWS, dtype=np.float64)) + pair(np.arange(24, dtype=np.float64) * ROWS)


class Net:
    def __init__(self, send, recv, core_send, core_recv, sibling, c):
        self.send, self.recv, self.core_send, self.core_recv = send, recv, core_send, core_recv
        self.sibling = sibling
        self.c = self.who = c
        self.count = 0
        self.sent = []
        self.shared = []

    def describe(self, region, i, peer):
        ref = region()
        return pltpu.make_async_remote_copy(
            src_ref=ref, dst_ref=ref, send_sem=self.send.at[i], recv_sem=self.recv.at[i],
            device_id=peer, device_id_type=pl.DeviceIdType.MESH)

    def put(self, region, peer):
        i = self.count
        self.count += 1
        self.describe(region, i, peer).start()
        self.sent.append((region, i, peer))
        return i

    def got(self, region, i):
        self.describe(region, i, self.sibling).wait_recv()

    def describe_core(self, region, i):
        ref = region()
        return pltpu.make_async_remote_copy(
            src_ref=ref, dst_ref=ref, send_sem=self.core_send.at[i], recv_sem=self.core_recv.at[i],
            device_id=self.sibling, device_id_type=pl.DeviceIdType.MESH)

    def core(self, region, group):
        i = len(self.shared)
        self.describe_core(region, i).start()
        self.shared.append((region, group))

    def core_in(self, group):
        self.who = 1 - self.c
        for i, (region, belongs) in enumerate(self.shared):
            if belongs == group:
                self.describe_core(region, i).wait_recv()
        self.who = self.c

    def finish(self):
        for region, i, peer in self.sent:
            self.describe(region, i, peer).wait_send()
        for i, (region, _) in enumerate(self.shared):
            self.describe_core(region, i).wait_send()


def ring(net, reg, half, plus, minus, here, before, after, across, core, core_last=None):
    ids = {}

    def first():
        ids["p"] = net.put(lambda: reg(here), plus)
        ids["m"] = net.put(lambda: reg(here), minus)

    def second():
        net.got(lambda: reg(before), ids["p"])
        net.got(lambda: reg(after), ids["m"])
        ids["pp"] = net.put(lambda: half(before, 0), plus)
        ids["mm"] = net.put(lambda: half(after, 1), minus)
        core(lambda: reg(before))
        core(lambda: reg(after))

    def third():
        net.got(lambda: half(across, 0), ids["pp"])
        net.got(lambda: half(across, 1), ids["mm"])
        (core_last or core)(lambda: reg(across))

    return [first, second, third]


def direct(net, reg, plus, minus, far, here, before, after, across, core):
    ids = {}

    def first():
        ids["p"] = net.put(lambda: reg(here), plus)
        ids["m"] = net.put(lambda: reg(here), minus)
        ids["f"] = net.put(lambda: reg(here), far)

    def second():
        net.got(lambda: reg(before), ids["p"])
        net.got(lambda: reg(after), ids["m"])
        core(lambda: reg(before))
        core(lambda: reg(after))
        net.got(lambda: reg(across), ids["f"])
        core(lambda: reg(across))

    return [first, second]


def chain(*rings):
    steps = list(rings[0])
    for following in rings[1:]:
        last = steps.pop()

        def joined(last=last, start=following[0]):
            last()
            start()

        steps.append(joined)
        steps.extend(following[1:])
    return steps


def beside(*lists):
    def step(k):
        def run():
            for steps in lists:
                steps[k]()
        return run
    return [step(k) for k in range(len(lists[0]))]


def kernel(lengths, resp, prompt, gain, wq, wk, wv, q_bias, k_bias, v_bias, wo, cos_b, sin_b, cos_a, sin_a,
           resid_out,
           x_resp, x_prompt, wq_all, wkv_all, wo_one, wo_mid, wo_two, kv_all, kv_own, q_all, attended, acc,
           send, recv, core_send, core_recv, att_send, att_recv, local, out_sem):
    g, s, t = lax.axis_index("group"), lax.axis_index("sample"), lax.axis_index("tensor")
    z, xh, c = s // 4, lax.rem(s // 2, 2), lax.rem(s, 2)
    x = 2 * xh + g

    def wrap(v):
        return lax.rem(v + 4, 4)

    def place(zz, xx, cc, tt):
        return (lax.rem(xx, 2), zz * 4 + (xx // 2) * 2 + cc, tt)

    zm, zp, z2 = wrap(z - 1), wrap(z + 1), wrap(z + 2)
    xm, xp, x2 = wrap(x - 1), wrap(x + 1), wrap(x + 2)
    tm, tp, t2 = wrap(t - 1), wrap(t + 1), wrap(t + 2)
    at_zp, at_zm = place(zp, x, c, t), place(zm, x, c, t)
    at_xp, at_xm, at_x2 = place(z, xp, c, t), place(z, xm, c, t), place(z, x2, c, t)
    at_z2, at_t2 = place(z2, x, c, t), place(z, x, c, t2)
    at_tp, at_tm = place(z, x, c, tp), place(z, x, c, tm)
    sibling = place(z, x, 1 - c, t)
    other = 1 - xh

    part = pl.ds(pl.multiple_of(g * 160, 160), 160)
    part_one = pl.ds(pl.multiple_of(g * 160, 160), ONE)
    part_mid = pl.ds(pl.multiple_of(g * 160 + ONE, 16), MID)
    part_two = pl.ds(pl.multiple_of(g * 160 + ONE + MID, 16), TWO)
    loads = [
        pltpu.make_async_copy(wk.at[part], wkv_all.at[c, z, xh, g, :, pl.ds(0, 128)], local.at[0]),
        pltpu.make_async_copy(wv.at[part], wkv_all.at[c, z, xh, g, :, pl.ds(128, 128)], local.at[1]),
        pltpu.make_async_copy(wq.at[part], wq_all.at[c, z, xh, g], local.at[2]),
        pltpu.make_async_copy(wo.at[part_one], wo_one.at[c, t, z, xh, g], local.at[3]),
        pltpu.make_async_copy(wo.at[part_two], wo_two.at[c, z, xh, g, t], local.at[4]),
        pltpu.make_async_copy(prompt, x_prompt, local.at[5]),
        pltpu.make_async_copy(resp, x_resp, local.at[6]),
        pltpu.make_async_copy(wo.at[part_mid], wo_mid.at[c, t, z, xh, g], local.at[8]),
    ]
    for load in loads:
        load.start()

    barrier = pltpu.get_barrier_semaphore()
    for peer in (at_zp, at_zm, at_z2, at_t2, at_xp, at_xm, at_x2, at_tp, at_tm, sibling):
        pl.semaphore_signal(barrier, inc=1, device_id=peer, device_id_type=pl.DeviceIdType.MESH)
    pl.semaphore_wait(barrier, 10)

    net = Net(send, recv, core_send, core_recv, sibling, c)

    def to_core(k):
        return lambda region: net.core(region, k)

    def rows_half(r0, count, which):
        low = count // 2 if count <= 4 else (count // 2 + 15) // 16 * 16
        return pl.ds(r0, low) if which == 0 else pl.ds(r0 + low, count - low)

    def halved(r0, count, cols, which):
        if count == 16:
            return pl.ds(r0, 16), pl.ds(0, 384) if which == 0 else pl.ds(384, 256)
        return rows_half(r0, count, which), cols

    def plane(reg, split_a, split_b, core, core_last=None, straight=(False, False)):
        (ra, na, ca), (rb, nb, cb) = split_a, split_b
        da, db = pl.ds(ra, na), pl.ds(rb, nb)
        where = {"m": (xm // 2, lax.rem(xm, 2)), "p": (xp // 2, lax.rem(xp, 2)), "h": (xh, g), "2": (x2 // 2, lax.rem(x2, 2))}

        def gather(stage, whole, half, axis):
            plus, minus, far, places = (at_zp, at_zm, at_z2, (z, zm, zp, z2)) if axis == "z" else (
                at_xp, at_xm, at_x2, ("h", "m", "p", "2"))
            if straight[stage]:
                return direct(net, whole, plus, minus, far, *places, core)
            return ring(net, whole, half, plus, minus, *places, core, core_last if stage else None)

        a1 = gather(0, lambda p: reg(p, xh, g, da, ca), lambda p, w: reg(p, xh, g, *halved(ra, na, ca, w)), "z")
        a2 = gather(1, lambda p: reg(ALL, *where[p], da, ca), lambda p, w: reg(pl.ds(2 * w, 2), *where[p], da, ca), "x")
        b1 = gather(0, lambda p: reg(z, *where[p], db, cb), lambda p, w: reg(z, *where[p], *halved(rb, nb, cb, w)), "x")
        b2 = gather(1, lambda p: reg(p, ALL, ALL, db, cb), lambda p, w: reg(p, pl.ds(w, 1), ALL, db, cb), "z")
        steps = beside(chain(a1, a2), chain(b1, b2))
        start = steps[0]

        def first():
            start()
            core(lambda: reg(z, xh, g, ALL, ALL))

        steps[0] = first
        return steps

    wkv_steps = plane(lambda zz, hh, gg, r, k: wkv_all.at[net.who, zz, hh, gg, r, k],
                      (0, 160, pl.ds(0, 128)), (0, 160, pl.ds(128, 128)), to_core(0), straight=(True, False))
    wq_steps = plane(lambda zz, hh, gg, r, k: wq_all.at[net.who, zz, hh, gg, r, k],
                     (0, 80, ALL), (80, 80, ALL), to_core(1))
    def plane_then_y(buf, split_a, split_b, k, k_last):
        return chain(
            plane(lambda zz, hh, gg, r, cols: buf.at[net.who, t, zz, hh, gg, r, cols], split_a, split_b, to_core(k)),
            ring(net, lambda p: buf.at[net.who, p], lambda p, w: buf.at[net.who, p, pl.ds(2 * w, 2)],
                 at_tp, at_tm, t, tm, tp, t2, to_core(k), to_core(k_last)))

    one_steps = plane_then_y(wo_one, (0, 16, ALL), (16, 16, ALL), 2, 6)
    mid_steps = plane_then_y(wo_mid, (0, MID, pl.ds(0, 256)), (0, MID, pl.ds(256, 384)), 7, 8)
    two_steps = chain(
        ring(net, lambda p: wo_two.at[net.who, z, xh, g, p],
             lambda p, w: wo_two.at[net.who, z, xh, g, p, rows_half(0, TWO, w)],
             at_tp, at_tm, t, tm, tp, t2, lambda region: None),
        plane(lambda zz, hh, gg, r, k: wo_two.at[net.who, zz, hh, gg, r],
              (0, 2, ALL), (2, 2, ALL), to_core(3), to_core(5)))

    ka, kb = pl.ds(0, 192), pl.ds(192, 320)
    kv_core = to_core(4)
    kv_ids = {}
    kv_za = ring(net, lambda p: kv_all.at[net.who, p, xh, ka], lambda p, w: kv_all.at[net.who, p, xh, pl.ds(96 * w, 96)],
                 at_zp, at_zm, z, zm, zp, z2, kv_core)
    kv_zb = ring(net, lambda p: kv_all.at[net.who, p, :, kb], lambda p, w: kv_all.at[net.who, p, pl.ds(w, 1), kb],
                 at_zp, at_zm, z, zm, zp, z2, kv_core)

    def kv_0():
        kv_za[0]()
        kv_ids["b"] = net.put(lambda: kv_all.at[net.who, z, xh, kb], at_x2)
        kv_core(lambda: kv_all.at[net.who, z, xh])

    def kv_1():
        kv_za[1]()
        net.got(lambda: kv_all.at[net.who, z, other, kb], kv_ids["b"])
        kv_core(lambda: kv_all.at[net.who, z, other, kb])
        kv_zb[0]()

    def kv_2():
        kv_za[2]()
        kv_ids["a"] = net.put(lambda: kv_all.at[net.who, :, xh, ka], at_x2)
        kv_zb[1]()

    def kv_3():
        net.got(lambda: kv_all.at[net.who, :, other, ka], kv_ids["a"])
        kv_core(lambda: kv_all.at[net.who, :, other, ka])
        kv_zb[2]()

    gain_row = gain[...].astype(F32).reshape(1, WIDTH)
    q_row = q_bias[...].astype(F32).reshape(1, Q_COLS)
    k_row = k_bias[...].astype(F32).reshape(1, HEAD)
    v_row = v_bias[...].astype(F32).reshape(1, HEAD)

    def normalize(ref, first, count):
        def rows32(i, _):
            r = pl.ds(pl.multiple_of(first + i * 32, 32), 32)
            v = ref[r, :].astype(F32)
            scale = lax.rsqrt(jnp.mean(v * v, axis=-1, keepdims=True) + EPS)
            ref[r, :] = (v * scale * gain_row).astype(BF16)
            return 0
        lax.fori_loop(0, count // 32, rows32, 0)

    def project(rows_ref, weights, width, first=0, last=4):
        if first == 0:
            acc[:, :width] = jnp.zeros((ROWS, width), F32)

        def block(zz, _):
            left = rows_ref[:, pl.ds(pl.multiple_of(zz * 1280, 1280), 1280)]
            right = jnp.concatenate(
                [weights[cc, zz, hh].reshape(320, width) for hh in range(2) for cc in range(2)], 0)
            acc[:, :width] += jnp.dot(left, right, preferred_element_type=F32)
            return 0
        lax.fori_loop(first, last, block, 0)

    def angles(block):
        ca, sa = cos_a[pl.ds(block, 1), :], sin_a[pl.ds(block, 1), :]
        cb, sb = cos_b[...], sin_b[...]
        lane = lax.broadcasted_iota(jnp.int32, (ROWS, HEAD), 1)
        sine = sa * cb + ca * sb
        return ca * cb - sa * sb, jnp.where(lane < HEAD // 2, -sine, sine)

    def rope(u, cosine, sine):
        return u * cosine + pltpu.roll(u, HEAD // 2, 1) * sine

    def keys_values(block):
        cosine, sine = angles(block)
        keys = rope(acc[:, 0:128] + k_row, cosine, sine).astype(BF16)
        return keys, (acc[:, 128:256] + v_row).astype(BF16)

    loads[3].wait()
    one_steps[0]()
    loads[7].wait()
    mid_steps[0]()
    loads[0].wait()
    loads[1].wait()
    wkv_steps[0]()
    one_steps[1]()
    loads[4].wait()
    two_steps[0]()
    loads[2].wait()
    wq_steps[0]()
    one_steps[2]()
    mid_steps[1]()
    wkv_steps[1]()
    two_steps[1]()
    loads[5].wait()
    normalize(x_prompt, 0, 256)
    one_steps[3]()
    mid_steps[2]()
    wq_steps[1]()
    one_steps[4]()
    wkv_steps[2]()
    mid_steps[3]()
    normalize(x_prompt, 256, 256)
    wq_steps[2]()
    loads[6].wait()
    normalize(x_resp, 0, 256)
    wkv_steps[3]()
    normalize(x_resp, 256, 256)
    mid_steps[4]()
    net.core_in(0)
    project(x_prompt, wkv_all, 256)
    keys, values = keys_values(s)
    kv_all[c, z, xh, :, 0:128] = keys
    kv_all[c, z, xh, :, 128:256] = values
    kv_0()
    two_steps[2]()
    kv_1()
    wq_steps[3]()
    project(x_resp, wkv_all, 256)
    keys, values = keys_values(16)
    kv_own[:, 0:128] = keys
    kv_own[:, 128:256] = values
    two_steps[3]()
    kv_2()
    one_steps[5]()
    wq_steps[4]()
    net.core_in(1)
    two_steps[4]()
    kv_3()
    mid_steps[5]()
    project(x_resp, wq_all, Q_COLS, 0, 2)
    project(x_resp, wq_all, Q_COLS, 2, 4)
    cosine, sine = angles(16)
    for h in range(Q_HEADS):
        cols = slice(h * HEAD, (h + 1) * HEAD)
        q = rope(acc[:, cols] + q_row[:, cols], cosine, sine)
        q_all[h] = (q * (math.log2(math.e) / math.sqrt(HEAD))).astype(BF16)
    reload = pltpu.make_async_copy(resp, x_resp, local.at[7])
    reload.start()
    one_steps[6]()
    net.core_in(4)

    length = lengths[0]

    def att_copy(h, k, region, peer):
        return pltpu.make_async_remote_copy(
            src_ref=region, dst_ref=region, send_sem=att_send.at[h, k], recv_sem=att_recv.at[h, k],
            device_id=peer, device_id_type=pl.DeviceIdType.MESH)

    def att_first(h):
        att_copy(h, 0, attended.at[t, h], at_tp).start()
        att_copy(h, 1, attended.at[t, h], at_tm).start()

    def att_second(h):
        att_copy(h, 0, attended.at[tm, h], at_tp).wait_recv()
        att_copy(h, 1, attended.at[tp, h], at_tm).wait_recv()
        att_copy(h, 2, attended.at[tm, h, pl.ds(0, 256)], at_tp).start()
        att_copy(h, 3, attended.at[tp, h, pl.ds(256, 256)], at_tm).start()

    def att_third(h):
        att_copy(h, 2, attended.at[t2, h, pl.ds(0, 256)], at_tp).wait_recv()
        att_copy(h, 3, attended.at[t2, h, pl.ds(256, 256)], at_tm).wait_recv()

    def att_sent(h):
        att_copy(h, 0, attended.at[t, h], at_tp).wait_send()
        att_copy(h, 1, attended.at[t, h], at_tm).wait_send()
        att_copy(h, 2, attended.at[tm, h, pl.ds(0, 256)], at_tp).wait_send()
        att_copy(h, 3, attended.at[tp, h, pl.ds(256, 256)], at_tm).wait_send()

    def head(h, _):
        q = q_all[h]

        def scores(j):
            k = kv_all[j // 2, pl.ds(2 * (j % 2), 2), :, :, 0:128].reshape(2048, HEAD)
            return lax.dot_general(q, k, NT, preferred_element_type=F32)

        def widened(v):
            return jnp.concatenate([v, jnp.ones_like(v)], 1)

        score = lax.dot_general(q, kv_own[:, 0:128], NT, preferred_element_type=F32)
        row = lax.broadcasted_iota(jnp.int32, (ROWS, ROWS), 0)
        col = lax.broadcasted_iota(jnp.int32, (ROWS, ROWS), 1)
        score = jnp.where(col <= row, score, -1e30)
        value = widened(kv_own[:, 128:256])
        highest = total = None
        for j in range(5):
            if j < 4:
                score_next = scores(j)
                value_next = widened(kv_all[j // 2, pl.ds(2 * (j % 2), 2), :, :, 128:256].reshape(2048, HEAD))
            top = jnp.max(score, axis=1, keepdims=True)
            fresh = top if j == 0 else jnp.maximum(highest, top)
            probs = jnp.exp2(score - fresh).astype(BF16)
            term = jnp.dot(probs, value, preferred_element_type=F32)
            total = term if j == 0 else total * jnp.exp2(highest - fresh) + term
            highest = fresh
            score, value = score_next, value_next
        live = lax.broadcasted_iota(jnp.int32, (ROWS, HEAD), 0) < length
        attended[t, h] = jnp.where(live, total[:, :HEAD] / total[:, HEAD:], 0.0).astype(BF16)
        att_first(h)

        @pl.when(h > 0)
        def _():
            att_second(h - 1)

        @pl.when(h == 1)
        def _():
            two_steps[5]()
            net.core_in(7)
            mid_steps[6]()

        @pl.when(h == 2)
        def _():
            net.core_in(2)

        @pl.when(h == 3)
        def _():
            net.core_in(3)
            two_steps[6]()
        return 0

    lax.fori_loop(0, Q_HEADS, head, 0)
    reload.wait()
    net.core_in(5)

    def out_copy(zz):
        cols = pl.ds(pl.multiple_of(zz * 1280, 1280), 1280)
        return pltpu.make_async_copy(x_prompt.at[:, cols], resid_out.at[:, cols], out_sem.at[zz])

    def branch(zz, pieces):
        left = jnp.concatenate([attended[tt, h] for tt, low, high in pieces for h in range(low, high)], 1)
        right = jnp.concatenate(
            [jnp.concatenate(
                [buf[:, low * HEAD:high * HEAD] for hh in range(2) for cc in range(2) for gg in range(2)
                 for buf in (wo_one.at[cc, tt, zz, hh, gg], wo_mid.at[cc, tt, zz, hh, gg],
                             wo_two.at[cc, zz, hh, gg, tt])], 0)
             for tt, low, high in pieces], 1)
        return lax.dot_general(left, right, NT, preferred_element_type=F32)

    def first_pass(zz, _):
        @pl.when(zz == 2)
        def _():
            att_second(Q_HEADS - 1)

        cols = pl.ds(pl.multiple_of(zz * 1280, 1280), 1280)
        term = branch(zz, [(t, 0, 4), (tm, 0, 4), (tp, 0, 4)])
        x_prompt[:, cols] = (x_resp[:, cols].astype(F32) + term).astype(BF16)
        return 0

    lax.fori_loop(0, 4, first_pass, 0)
    for h in range(Q_HEADS):
        att_third(h)
    net.core_in(8)
    net.core_in(6)

    def second_pass(zz, _):
        cols = pl.ds(pl.multiple_of(zz * 1280, 1280), 1280)
        term = branch(zz, [(t2, 0, 5), (t, 4, 5), (tm, 4, 5), (tp, 4, 5)])
        x_prompt[:, cols] = (x_prompt[:, cols].astype(F32) + term).astype(BF16)
        out_copy(zz).start()
        return 0

    lax.fori_loop(0, 4, second_pass, 0)

    net.finish()
    for h in range(Q_HEADS):
        att_sent(h)
    for zz in range(4):
        out_copy(zz).wait()


def finish_kernel(lengths, resid, gain, mixed):
    rows = resid.shape[0]
    v = resid[...].astype(F32)
    scale = lax.rsqrt(jnp.mean(v * v, axis=-1, keepdims=True) + EPS)
    slot = pl.program_id(0) * rows + lax.broadcasted_iota(jnp.int32, (rows, 1), 0)
    out = v * scale * gain[...].astype(F32).reshape(1, WIDTH)
    mixed[...] = jnp.where(slot < lengths[0], out, 0.0).astype(BF16)


def on_device(resp_hidden, prompt_hidden, lengths, norm_gain, wq, wk, wv, q_bias, k_bias, value_bias, wo_t, post_gain):
    resp = resp_hidden[0]
    tables = [jnp.asarray(a) for a in rope_tables()]
    vmem = pl.BlockSpec(memory_space=pltpu.VMEM)
    hbm = pl.BlockSpec(memory_space=pl.ANY)
    smem = pl.BlockSpec(memory_space=pltpu.SMEM)
    dma = pltpu.SemaphoreType.DMA
    resid = pl.pallas_call(
        kernel,
        out_shape=jax.ShapeDtypeStruct((ROWS, WIDTH), BF16),
        in_specs=[smem, hbm, hbm, vmem, hbm, hbm, hbm, vmem, vmem, vmem, hbm, vmem, vmem, vmem, vmem],
        out_specs=hbm,
        scratch_shapes=[
            pltpu.VMEM((ROWS, WIDTH), BF16),
            pltpu.VMEM((ROWS, WIDTH), BF16),
            pltpu.VMEM((2, 4, 2, 2, 160, Q_COLS), BF16),
            pltpu.VMEM((2, 4, 2, 2, 160, 256), BF16),
            pltpu.VMEM((2, 4, 4, 2, 2, ONE, Q_COLS), BF16),
            pltpu.VMEM((2, 4, 4, 2, 2, MID, Q_COLS), BF16),
            pltpu.VMEM((2, 4, 2, 2, 4, TWO, Q_COLS), BF16),
            pltpu.VMEM((2, 4, 2, ROWS, 256), BF16),
            pltpu.VMEM((ROWS, 256), BF16),
            pltpu.VMEM((Q_HEADS, ROWS, HEAD), BF16),
            pltpu.VMEM((4, Q_HEADS, ROWS, HEAD), BF16),
            pltpu.VMEM((ROWS, Q_COLS), F32),
            dma((110,)), dma((110,)), dma((90,)), dma((90,)), dma((Q_HEADS, 4)), dma((Q_HEADS, 4)), dma((9,)), dma((4,)),
        ],
        compiler_params=pltpu.CompilerParams(
            collective_id=0, has_side_effects=True, vmem_limit_bytes=67000000),
        cost_estimate=pl.CostEstimate(flops=31_000_000_000, bytes_accessed=30_000_000, transcendentals=22_000_000),
    )(lengths, resp, prompt_hidden, norm_gain, wq, wk, wv, q_bias, k_bias, value_bias, wo_t,
      *tables)
    block = pl.BlockSpec((128, WIDTH), lambda i: (i, 0))
    mixed = pl.pallas_call(
        finish_kernel,
        out_shape=jax.ShapeDtypeStruct((ROWS, WIDTH), BF16),
        grid=(ROWS // 128,),
        in_specs=[smem, block, vmem],
        out_specs=block,
    )(lengths, resid, post_gain)
    return mixed[None]


def solution(mesh):
    placed = (
        P(("group", "sample"), None, None),
        P(("group", "sample"), None),
        P(("group", "sample")),
        P(),
        P("sample", "tensor"),
        P("sample", "tensor"),
        P("sample", "tensor"),
        P("tensor"),
        P("tensor"),
        P("tensor"),
        P("sample", "tensor"),
        P(),
    )
    return jax.shard_map(
        on_device,
        mesh=mesh,
        in_specs=placed,
        out_specs=P(("group", "sample"), None, None),
        check_vma=False,
    )
```
